32 devices in a mesh: grp: 4 (over x, core), sub: 8 (over z, y).
Axes of the slice: x: 2, y: 2, z: 4, core: 2. Of those that a mesh axis runs over, the one named last changes fastest.
Arguments:
- right_side: float32 [65536, 128], P(('grp', 'sub')), may hold values from -6 to 6
- fine_values: float32 [81, 65536], P(None, ('grp', 'sub')), as said below
- columns: int32 [81, 65536], P(None, ('grp', 'sub')), may hold values from 0 to 2175, as said below
- agg_map: int32 [65536], P(('grp', 'sub')), may hold values from 0 to 127
- send_lo: int32 [2048], P(('grp', 'sub')), may hold values from 0 to 2047
- send_hi: int32 [2048], P(('grp', 'sub')), may hold values from 0 to 2047
- coarse_matrix: float32 [4, 1024, 1024], P('grp', 'sub'), as said below
Outputs:
- solution: float32 [65536, 128], P(('grp', 'sub'))
- residual: float32 [65536, 128], P(('grp', 'sub'))
The draws below stay inside these ranges and needn't reach their ends.
Inputs may be any that keep to these rules, and one draw needn't show every extreme that they name: `columns`: entry 0 of row i of a partition is 64 + i, the others lie within 64 positions of it. `fine_values`: entry 0 lies in 2.5 to 5 and every other entry's magnitude is at most 0.06. `coarse_matrix`: symmetric; the diagonal lies in 10 to 20, other entries' magnitudes are at most 7.1 / sqrt(1024).
All inputs are finite; a program needn't handle non-finite values.
Results may differ from the reference program's by a relative error of at most 0.0001.
Values sent between devices are 32-bit elements; how exact they have to be, the bound alone decides.
A program may use at most 128 MiB of HBM per device.

```python
import jax
import jax.numpy as jnp
from jax import lax

ROWS_DEV = 2048
NRHS = 128
STENCIL = 81
GHOST = 64
AGG_SIZE = 16
CHEB_FINE = 2
CHEB_COARSE = 6
CYCLES = 2
BLOCK = 128
AGG = 128
COARSE = 1024
ROWS = 65536
N_GRP = 4
DEVICES = 32


def draw_columns(key, part):
    rows = jnp.arange(ROWS, dtype=jnp.int32) % ROWS_DEV
    offsets = jax.random.randint(key, (STENCIL, ROWS), -GHOST, GHOST + 1, dtype=jnp.int32)
    entry = jnp.arange(STENCIL, dtype=jnp.int32)[:, None]
    offsets = jnp.where(entry == 0, 0, offsets)
    offsets = jnp.where((entry == 1) & (rows[None, :] == 0), -GHOST, offsets)
    offsets = jnp.where((entry == 1) & (rows[None, :] == ROWS_DEV - 1), GHOST, offsets)
    return (GHOST + rows[None, :] + offsets).astype(jnp.int32)


def draw_fine_values(key, part):
    diagonal = jax.random.uniform(jax.random.fold_in(key, 1), (1, ROWS), jnp.float32, 2.5, 5.0)
    others = jax.random.uniform(jax.random.fold_in(key, 2), (STENCIL, ROWS), jnp.float32, -0.06, 0.06)
    entry = jnp.arange(STENCIL, dtype=jnp.int32)[:, None]
    return jnp.where(entry == 0, diagonal, others)


def draw_agg_map(key, part):
    rows = jnp.arange(ROWS, dtype=jnp.int32) % ROWS_DEV
    base = rows // AGG_SIZE
    moved = jax.random.randint(jax.random.fold_in(key, 3), (ROWS,), 0, AGG, dtype=jnp.int32)
    select = jax.random.randint(jax.random.fold_in(key, 4), (ROWS,), 0, 4, dtype=jnp.int32)
    return jnp.where(select == 0, moved, base).astype(jnp.int32)


def draw_coarse_matrix(key, part):
    bound = 5.0 / jnp.sqrt(jnp.float32(COARSE))
    table = jax.random.uniform(jax.random.fold_in(key, 5), (N_GRP, COARSE, COARSE), jnp.float32, -1.0, 1.0) * bound
    others = (table + jnp.swapaxes(table, 1, 2)) * 0.70710677
    diagonal = jax.random.uniform(jax.random.fold_in(key, 6), (N_GRP, COARSE, 1), jnp.float32, 10.0, 20.0)
    rows = jnp.arange(COARSE, dtype=jnp.int32)
    same = rows[:, None] == rows[None, :]
    return jnp.where(same[None, :, :], diagonal, others)


def place_ends(values, key, least, top_value):
    longest = values.shape.index(max(values.shape))
    spots = []
    for shift in (0, 1):
        where = [jax.random.randint(jax.random.fold_in(key, axis), (), 0, length) for axis, length in enumerate(values.shape)]
        where[longest] = (where[longest] + shift) % values.shape[longest]
        spots.append(tuple(where))
    return values.at[spots[0]].set(least).at[spots[1]].set(top_value)


def block_levels(rng, shape, cuts, low, largest):
    loudness = 1.0
    for axis_at, blocks in cuts:
        draws = jax.random.uniform(jax.random.fold_in(jax.random.fold_in(rng, 6), axis_at), (blocks,), jnp.float32, low / len(cuts), largest / len(cuts))
        loudness = loudness * jnp.repeat(jnp.exp(draws), shape[axis_at] // blocks).reshape((-1,) + (1,) * (len(shape) - 1 - axis_at))
    return loudness


def normal_values(stream_key, shape, scale, most, split=(), kind=jnp.bfloat16):
    gain = block_levels(stream_key, shape, split, -0.22, 0.18) if split else 1.0
    entries = jax.random.normal(stream_key, shape, jnp.float32) * scale * gain
    return jnp.minimum(jnp.maximum(entries, -most), most).astype(kind)


def setup_inputs(seed: int = 0) -> dict:
    streams_of = jax.random.split(jax.random.key(seed), 8)
    right_side = normal_values(streams_of[0], (ROWS, NRHS), 1.0, 6.0, ((0, 32),), jnp.float32)
    fine_values = draw_fine_values(jax.random.fold_in(streams_of[7], 71), 0)
    columns = draw_columns(jax.random.fold_in(streams_of[7], 71), 0)
    agg_map = draw_agg_map(jax.random.fold_in(streams_of[7], 71), 0)
    send_lo = place_ends(jax.random.randint(streams_of[4], (DEVICES * GHOST,), 0, ROWS_DEV), jax.random.fold_in(streams_of[4], 1), 0, ROWS_DEV - 1).astype(jnp.int32)
    send_hi = place_ends(jax.random.randint(streams_of[5], (DEVICES * GHOST,), 0, ROWS_DEV), jax.random.fold_in(streams_of[5], 1), 0, ROWS_DEV - 1).astype(jnp.int32)
    coarse_matrix = draw_coarse_matrix(jax.random.fold_in(streams_of[7], 71), 0)
    return {"right_side": right_side, "fine_values": fine_values, "columns": columns, "agg_map": agg_map, "send_lo": send_lo, "send_hi": send_hi, "coarse_matrix": coarse_matrix}


THETA = 1.0
DELTA = 0.7
OMEGA = 0.6
highest = lax.Precision.HIGHEST


def picker(table, index):
    return jax.vmap(lambda source, where: jnp.take(source, where, axis=0))(table, index)


def band_tiles(fine_values, columns):
    rows = jnp.arange(ROWS_DEV, dtype=jnp.int32)
    starts = (rows // BLOCK) * BLOCK
    index_all = columns.reshape(STENCIL, DEVICES, ROWS_DEV)
    flat = rows[None, None, :] * (2 * BLOCK) + index_all - starts[None, None, :]
    offsets = jnp.arange(DEVICES, dtype=jnp.int32) * (ROWS_DEV * 2 * BLOCK)
    flat = (flat + offsets[None, :, None]).astype(jnp.int32)
    tiles = jnp.zeros((DEVICES * ROWS_DEV * 2 * BLOCK,), jnp.float32)
    tiles = tiles.at[flat.reshape(-1)].add(fine_values.reshape(-1))
    tiles = tiles.reshape(DEVICES, ROWS_DEV // BLOCK, BLOCK, 2 * BLOCK)
    return tiles[:, :, :, :BLOCK], tiles[:, :, :, BLOCK:]


def fine_apply(vector, low_tiles, high_tiles, send_lo, send_hi):
    blocks = vector.reshape(DEVICES, ROWS_DEV, NRHS)
    upper_rows = picker(blocks, send_hi.reshape(DEVICES, GHOST))
    lower_rows = picker(blocks, send_lo.reshape(DEVICES, GHOST))
    empty = jnp.zeros((1, GHOST, NRHS), jnp.float32)
    below = jnp.concatenate([empty, upper_rows[:-1]], 0)
    above = jnp.concatenate([lower_rows[1:], empty], 0)
    extended = jnp.concatenate([below, blocks, above], 1)
    pieces = extended.reshape(DEVICES, ROWS_DEV // BLOCK + 1, BLOCK, NRHS)
    total = jnp.einsum('dbrc,dbcn->dbrn', low_tiles, pieces[:, :-1], precision=highest)
    total = total + jnp.einsum('dbrc,dbcn->dbrn', high_tiles, pieces[:, 1:], precision=highest)
    return total.reshape(ROWS, NRHS)


def chebyshev(residual, apply, inverse, steps, final):
    rho_old = DELTA / THETA
    direction = inverse * residual / THETA
    result = direction
    for turn in range(1, steps):
        residual = residual - apply(direction)
        rho_new = 1.0 / (2.0 * THETA / DELTA - rho_old)
        direction = rho_new * rho_old * direction + (2.0 * rho_new / DELTA) * inverse * residual
        result = result + direction
        rho_old = rho_new
    if final:
        residual = residual - apply(direction)
    return result, residual


def reference(right_side, fine_values, columns, agg_map, send_lo, send_hi, coarse_matrix):
    low_tiles, high_tiles = band_tiles(fine_values, columns)

    def apply_fine(vector):
        return fine_apply(vector, low_tiles, high_tiles, send_lo, send_hi)

    def apply_coarse(vector):
        return jnp.einsum('gij,gjn->gin', coarse_matrix, vector, precision=highest)

    dinv = 1.0 / fine_values[0][:, None]
    cinv = 1.0 / jnp.diagonal(coarse_matrix, axis1=1, axis2=2)[:, :, None]
    maps = agg_map.reshape(DEVICES, ROWS_DEV)
    onehot = (maps[:, :, None] == jnp.arange(AGG, dtype=jnp.int32)[None, None, :]).astype(jnp.float32)
    solution = jnp.zeros_like(right_side)
    residual = right_side
    for cycle in range(CYCLES):
        update, residual = chebyshev(residual, apply_fine, dinv, CHEB_FINE, True)
        solution = solution + update
        smoothed = residual - OMEGA * apply_fine(dinv * residual)
        coarse_rhs = jnp.einsum('dra,drn->dan', onehot, smoothed.reshape(DEVICES, ROWS_DEV, NRHS), precision=highest)
        coarse_rhs = coarse_rhs.reshape(N_GRP, COARSE, NRHS)
        coarse_corr, unused = chebyshev(coarse_rhs, apply_coarse, cinv, CHEB_COARSE, False)
        spread = picker(coarse_corr.reshape(DEVICES, AGG, NRHS), maps).reshape(ROWS, NRHS)
        correction = spread - OMEGA * dinv * apply_fine(spread)
        solution = solution + correction
        residual = residual - apply_fine(correction)
        update, residual = chebyshev(residual, apply_fine, dinv, CHEB_FINE, True)
        solution = solution + update
    return solution, residual
```

```python
import functools

import jax
import jax.numpy as jnp
from jax import lax
from jax.experimental import pallas as pl
from jax.experimental.pallas import tpu as pltpu
from jax.sharding import PartitionSpec as P

CHEB_FINE = 2
CHEB_COARSE = 6
CYCLES = 2
APPLIES = 7

THETA = 1.0
DELTA = 0.7
OMEGA = 0.6
MESH = pl.DeviceIdType.MESH
f32 = jnp.float32
bf16 = jnp.bfloat16


def split(x):
    hi = x.astype(bf16)
    lo = (x - hi.astype(f32)).astype(bf16)
    return hi, lo


def iota(shape, dim):
    return lax.broadcasted_iota(jnp.int32, shape, dim)


def setup_kernel(fv_ref, col_ref, agg_ref, a_ref, dinv_ref, diag_ref, oht_ref, oh_ref):
    block = fv_ref.shape[1]
    count = fv_ref.shape[0] - 1
    groups = count // 8
    base = pl.program_id(0) * block
    rows = iota((8, block), 1)
    cols, vals, firsts = [], [], []
    for i in range(groups):
        cols.append(col_ref[1 + 8 * i : 9 + 8 * i, :] - base - rows)
        vals.append(fv_ref[1 + 8 * i : 9 + 8 * i, :])
    last = jnp.zeros((8, block), f32)
    for i in range(groups):
        last = last + jnp.where(cols[i] == block, vals[i], 0.0)
    last = jnp.sum(last, axis=0, keepdims=True)
    for j in range(groups):
        total = vals[j]
        for i in range(j + 1, groups):
            total = total + jnp.where(cols[i] == cols[j], vals[i], 0.0)
        firsts.append(total)
    high_count = block // 8
    places = [iota((8, block), 0) + 8 * h for h in range(high_count)]
    sums = [jnp.zeros((8, block), f32)] * high_count
    for s in range(8):
        chains = [jnp.zeros((8, block), f32)] * high_count
        for i in reversed(range(groups)):
            col = jnp.broadcast_to(cols[i][s : s + 1, :], (8, block))
            val = jnp.broadcast_to(firsts[i][s : s + 1, :], (8, block))
            chains = [jnp.where(col == places[h], val, chains[h]) for h in range(high_count)]
        sums = [sums[h] + chains[h] for h in range(high_count)]
    by_offset = jnp.concatenate(sums, axis=0).T
    skewed = pltpu.roll(by_offset, 0, 1, stride=1, stride_axis=0)
    lane = iota((block, block), 1)
    sub = iota((block, block), 0)
    low = jnp.where(lane >= sub, skewed, 0.0)
    high = jnp.where(lane < sub, skewed, jnp.where(lane == sub, last, 0.0))
    for part, at in ((low, 0), (high, block)):
        hi, lo = split(part)
        a_ref[:block, at : at + block] = hi
        a_ref[block:, at : at + block] = lo
    diag = jnp.broadcast_to(fv_ref[0:1, :], (block, block)).T
    diag_ref[...] = diag
    dinv_ref[...] = 1.0 / diag
    count_agg = oht_ref.shape[0]
    onehot = (iota((count_agg, block), 0) == agg_ref[...]).astype(f32)
    oht_ref[...] = onehot.astype(bf16)
    oh_ref[...] = onehot.T.astype(bf16)


def run_setup(fine_values, columns, agg_map, block, aggregates):
    entries, rows = fine_values.shape
    blocks = rows // block
    return pl.pallas_call(
        setup_kernel,
        grid=(blocks,),
        in_specs=[
            pl.BlockSpec((entries, block), lambda b: (0, b)),
            pl.BlockSpec((entries, block), lambda b: (0, b)),
            pl.BlockSpec((1, block), lambda b: (0, b)),
        ],
        out_specs=[
            pl.BlockSpec((2 * block, 2 * block), lambda b: (b, 0)),
            pl.BlockSpec((block, block), lambda b: (b, 0)),
            pl.BlockSpec((block, block), lambda b: (b, 0)),
            pl.BlockSpec((aggregates, block), lambda b: (0, b)),
            pl.BlockSpec((block, aggregates), lambda b: (b, 0)),
        ],
        out_shape=[
            jax.ShapeDtypeStruct((2 * rows, 2 * block), bf16),
            jax.ShapeDtypeStruct((rows, block), f32),
            jax.ShapeDtypeStruct((rows, block), f32),
            jax.ShapeDtypeStruct((aggregates, rows), bf16),
            jax.ShapeDtypeStruct((rows, aggregates), bf16),
        ],
        name="setup",
    )(fine_values, columns, agg_map.reshape(1, rows))


def quads(product, rows, width):
    return product[:rows, :width] + (product[:rows, width:] + product[rows:, :width])


def main_kernel(
    n_grp, n_sub,
    rhs_ref, a_ref, dinv_ref, diag_ref, oht_ref, oh_ref, lo_ref, hi_ref, coarse_ref,
    sol_ref, res_ref,
    xs, ext, s2, m2, send, recv, csend, whole, send_sem, recv_sem, csend_sem, crecv_sem,
):
    rows_dev, width = rhs_ref.shape
    ghost = lo_ref.shape[0]
    block = 2 * ghost
    blocks = rows_dev // block
    agg = coarse_ref.shape[0]
    grp = lax.axis_index("grp")
    me = lax.axis_index("sub")
    part = grp * n_sub + me
    has_next = part < n_grp * n_sub - 1
    has_prev = part > 0
    after, before = part + 1, part - 1
    next_id = (lax.div(after, n_sub), lax.rem(after, n_sub))
    prev_id = (lax.div(before, n_sub), lax.rem(before, n_sub))
    cross_next = jnp.logical_and(has_next, me == n_sub - 1)
    cross_prev = jnp.logical_and(has_prev, me == 0)

    barrier = pltpu.get_barrier_semaphore()
    for j in range(1, n_sub):
        pl.semaphore_signal(barrier, inc=1, device_id=(grp, lax.rem(me + j, n_sub)), device_id_type=MESH)

    @pl.when(cross_next)
    def _():
        pl.semaphore_signal(barrier, inc=1, device_id=next_id, device_id_type=MESH)

    @pl.when(cross_prev)
    def _():
        pl.semaphore_signal(barrier, inc=1, device_id=prev_id, device_id_type=MESH)

    own = coarse_ref[...]
    hi, lo = split(own)
    m2[:agg, :] = hi
    m2[agg:, :] = lo
    mine = pl.multiple_of(me * agg, agg)
    center = coarse_ref[:, pl.ds(mine, agg)]
    eye = iota((agg, agg), 0) == iota((agg, agg), 1)
    cinv = 1.0 / jnp.sum(jnp.where(eye, center, 0.0), axis=1, keepdims=True)
    cinv = jnp.broadcast_to(cinv, (agg, width))
    ext[:ghost, :] = jnp.zeros((ghost, 2 * width), bf16)
    ext[ghost + rows_dev :, :] = jnp.zeros((ghost, 2 * width), bf16)

    def each_block(fn):
        def go(b, carry):
            fn(pl.ds(pl.multiple_of(b * block, block), block))
            return carry
        lax.fori_loop(0, blocks, go, 0, unroll=True)

    def first(sl):
        rhs = rhs_ref[sl, :]
        res_ref[sl, :] = rhs
        sol_ref[sl, :] = jnp.zeros_like(rhs)
        xs[0, sl, :] = dinv_ref[sl, :] * rhs

    each_block(first)
    pl.semaphore_wait(barrier, n_sub - 1 + cross_next.astype(jnp.int32) + cross_prev.astype(jnp.int32))

    def halo_copy(ex, way, device):
        return pltpu.make_async_remote_copy(
            src_ref=send.at[ex, way], dst_ref=recv.at[ex, way],
            send_sem=send_sem.at[ex, way], recv_sem=recv_sem.at[ex, way],
            device_id=device, device_id_type=MESH,
        )

    def apply(ex, cur, epilogue):
        up = halo_copy(ex, 0, next_id)
        down = halo_copy(ex, 1, prev_id)

        @pl.when(has_next)
        def _():
            for i in range(ghost):
                send[ex, 0, i : i + 1, :] = xs[cur, pl.ds(hi_ref[i], 1), :]
            up.start()

        @pl.when(has_prev)
        def _():
            for i in range(ghost):
                send[ex, 1, i : i + 1, :] = xs[cur, pl.ds(lo_ref[i], 1), :]
            down.start()

        for b in range(blocks):
            hi, lo = split(xs[cur, b * block : (b + 1) * block, :])
            at = ghost + b * block
            ext[at : at + block, :width] = hi
            ext[at : at + block, width:] = lo

        def one(b):
            a = a_ref[pl.ds(pl.multiple_of(b * 2 * block, 2 * block), 2 * block), :]
            x = ext[pl.ds(pl.multiple_of(b * block, block), 2 * block), :]
            off = quads(jnp.dot(a, x, preferred_element_type=f32), block, width)
            epilogue(pl.ds(pl.multiple_of(b * block, block), block), off)

        def go(b, carry):
            one(1 + 2 * b)
            one(2 + 2 * b)
            return carry

        lax.fori_loop(0, (blocks - 2) // 2, go, 0)

        @pl.when(has_next)
        def _():
            down.wait_recv()
            hi, lo = split(recv[ex, 1])
            ext[ghost + rows_dev :, :width] = hi
            ext[ghost + rows_dev :, width:] = lo
            up.wait_send()

        @pl.when(has_prev)
        def _():
            up.wait_recv()
            hi, lo = split(recv[ex, 0])
            ext[:ghost, :width] = hi
            ext[:ghost, width:] = lo
            down.wait_send()

        one(0)
        one(blocks - 1)

    def gather(step, value):
        csend[step] = value
        copies = []
        for j in range(1, n_sub):
            copies.append(pltpu.make_async_remote_copy(
                src_ref=csend.at[step], dst_ref=whole.at[step, pl.ds(mine, agg)],
                send_sem=csend_sem.at[step, j], recv_sem=crecv_sem.at[step, j],
                device_id=(grp, lax.rem(me + j, n_sub)), device_id_type=MESH,
            ))
        for copy in copies:
            copy.start()
        whole[step, pl.ds(mine, agg), :] = value
        for copy in copies:
            copy.wait()
        hi, lo = split(whole[step])
        x = jnp.concatenate([hi, lo], axis=1)
        return quads(jnp.dot(m2[...], x, preferred_element_type=f32), agg, width)

    rho0 = DELTA / THETA
    rho1 = 1.0 / (2.0 * THETA / DELTA - rho0)
    c1 = rho1 * rho0
    c2 = 2.0 * rho1 / DELTA

    def smooth(ex):
        def step_one(sl, off):
            d0 = xs[0, sl, :]
            r0 = res_ref[sl, :]
            d1 = c1 * d0 - c2 * dinv_ref[sl, :] * off
            xs[1, sl, :] = d1
            res_ref[sl, :] = (c2 - 1.0) * off - c1 * r0
            sol_ref[sl, :] += d0 + d1

        apply(ex, 0, step_one)

        def step_two(sl, off):
            r = res_ref[sl, :] - off
            res_ref[sl, :] = r
            xs[0, sl, :] = dinv_ref[sl, :] * r

        apply(ex + 1, 1, step_two)

    def cycle_body(cycle, carry):
        ex = cycle * APPLIES
        smooth(ex)

        def restrict(sl, off):
            s = (1.0 - OMEGA) * res_ref[sl, :] - OMEGA * off
            hi, lo = split(s)
            s2[sl, :width] = hi
            s2[sl, width:] = lo

        apply(ex + 2, 0, restrict)
        both = jnp.dot(oht_ref[...], s2[...], preferred_element_type=f32)
        r = both[:, :width] + both[:, width:]
        d = cinv * r
        result = d
        rho_old = rho0
        for turn in range(1, CHEB_COARSE):
            r = r - gather(cycle * (CHEB_COARSE - 1) + turn - 1, d)
            rho_new = 1.0 / (2.0 * THETA / DELTA - rho_old)
            d = rho_new * rho_old * d + (2.0 * rho_new / DELTA) * (cinv * r)
            result = result + d
            rho_old = rho_new
        hi, lo = split(result)
        packed = jnp.concatenate([hi, lo], axis=1)

        def spread(sl):
            both = jnp.dot(oh_ref[sl, :], packed, preferred_element_type=f32)
            xs[0, sl, :] = both[:, :width] + both[:, width:]

        each_block(spread)

        def prolong(sl, off):
            e = (1.0 - OMEGA) * xs[0, sl, :] - OMEGA * (dinv_ref[sl, :] * off)
            xs[1, sl, :] = e
            sol_ref[sl, :] += e

        apply(ex + 3, 0, prolong)

        def correct(sl, off):
            r = res_ref[sl, :] - (diag_ref[sl, :] * xs[1, sl, :] + off)
            res_ref[sl, :] = r
            xs[0, sl, :] = dinv_ref[sl, :] * r

        apply(ex + 4, 1, correct)
        smooth(ex + 5)
        return carry

    lax.fori_loop(0, CYCLES, cycle_body, 0)


def body(n_grp, n_sub, right_side, fine_values, columns, agg_map, send_lo, send_hi, coarse_matrix):
    rows, width = right_side.shape
    ghost = send_lo.shape[0]
    block = 2 * ghost
    own = coarse_matrix[0]
    agg, coarse = own.shape
    a2, dinv, diag, oht, oh = run_setup(fine_values, columns, agg_map, block, agg)
    exchanges = CYCLES * APPLIES
    gathers = CYCLES * (CHEB_COARSE - 1)
    vmem = pl.BlockSpec(memory_space=pltpu.VMEM)
    smem = pl.BlockSpec(memory_space=pltpu.SMEM)
    return pl.pallas_call(
        functools.partial(main_kernel, n_grp, n_sub),
        in_specs=[vmem] * 6 + [smem] * 2 + [vmem],
        out_specs=[vmem] * 2,
        out_shape=[jax.ShapeDtypeStruct((rows, width), f32)] * 2,
        scratch_shapes=[
            pltpu.VMEM((2, rows, width), f32),
            pltpu.VMEM((rows + block, 2 * width), bf16),
            pltpu.VMEM((rows, 2 * width), bf16),
            pltpu.VMEM((2 * agg, coarse), bf16),
            pltpu.VMEM((exchanges, 2, ghost, width), f32),
            pltpu.VMEM((exchanges, 2, ghost, width), f32),
            pltpu.VMEM((gathers, agg, width), f32),
            pltpu.VMEM((gathers, coarse, width), f32),
            pltpu.SemaphoreType.DMA((exchanges, 2)),
            pltpu.SemaphoreType.DMA((exchanges, 2)),
            pltpu.SemaphoreType.DMA((gathers, n_sub)),
            pltpu.SemaphoreType.DMA((gathers, n_sub)),
        ],
        compiler_params=pltpu.CompilerParams(
            collective_id=0, has_side_effects=True, vmem_limit_bytes=50 * 1024 * 1024
        ),
        name="cycles",
    )(right_side, a2, dinv, diag, oht, oh, send_lo, send_hi, own)


def solution(mesh):
    placed = (
        P(("grp", "sub"), None),
        P(None, ("grp", "sub")),
        P(None, ("grp", "sub")),
        P(("grp", "sub")),
        P(("grp", "sub")),
        P(("grp", "sub")),
        P("grp", "sub", None),
    )
    return jax.shard_map(
        functools.partial(body, mesh.shape["grp"], mesh.shape["sub"]),
        mesh=mesh,
        in_specs=placed,
        out_specs=(P(("grp", "sub"), None), P(("grp", "sub"), None)),
        check_vma=False,
    )
```

```python
import functools

import jax
import jax.numpy as jnp
from jax import lax
from jax.experimental import pallas as pl
from jax.experimental.pallas import tpu as pltpu
from jax.sharding import PartitionSpec as P

CHEB_FINE = 2
CHEB_COARSE = 6
CYCLES = 2
APPLIES = 7

THETA = 1.0
DELTA = 0.7
OMEGA = 0.6
MESH = pl.DeviceIdType.MESH
f32 = jnp.float32
bf16 = jnp.bfloat16


def split(x):
    hi = x.astype(bf16)
    lo = (x - hi.astype(f32)).astype(bf16)
    return hi, lo


def iota(shape, dim):
    return lax.broadcasted_iota(jnp.int32, shape, dim)


def setup_kernel(fv_ref, col_ref, agg_ref, a_ref, dinv_ref, diag_ref, oht_ref, oh_ref):
    block = fv_ref.shape[1]
    count = fv_ref.shape[0] - 1
    groups = count // 8
    base = pl.program_id(0) * block
    rows = iota((8, block), 1)
    cols, vals, firsts = [], [], []
    for i in range(groups):
        cols.append(col_ref[1 + 8 * i : 9 + 8 * i, :] - base - rows)
        vals.append(fv_ref[1 + 8 * i : 9 + 8 * i, :])
    last = jnp.zeros((8, block), f32)
    for i in range(groups):
        last = last + jnp.where(cols[i] == block, vals[i], 0.0)
    last = jnp.sum(last, axis=0, keepdims=True)
    for j in range(groups):
        total = vals[j]
        for i in range(j + 1, groups):
            total = total + jnp.where(cols[i] == cols[j], vals[i], 0.0)
        firsts.append(total)
    high_count = block // 8
    places = [iota((8, block), 0) + 8 * h for h in range(high_count)]
    sums = [jnp.zeros((8, block), f32)] * high_count
    for s in range(8):
        chains = [jnp.zeros((8, block), f32)] * high_count
        for i in reversed(range(groups)):
            col = jnp.broadcast_to(cols[i][s : s + 1, :], (8, block))
            val = jnp.broadcast_to(firsts[i][s : s + 1, :], (8, block))
            chains = [jnp.where(col == places[h], val, chains[h]) for h in range(high_count)]
        sums = [sums[h] + chains[h] for h in range(high_count)]
    by_offset = jnp.concatenate(sums, axis=0).T
    skewed = pltpu.roll(by_offset, 0, 1, stride=1, stride_axis=0)
    lane = iota((block, block), 1)
    sub = iota((block, block), 0)
    low = jnp.where(lane >= sub, skewed, 0.0)
    high = jnp.where(lane < sub, skewed, jnp.where(lane == sub, last, 0.0))
    for part, at in ((low, 0), (high, block)):
        hi, lo = split(part)
        a_ref[:block, at : at + block] = hi
        a_ref[block:, at : at + block] = lo
    diag = jnp.broadcast_to(fv_ref[0:1, :], (block, block)).T
    diag_ref[...] = diag
    dinv_ref[...] = 1.0 / diag
    count_agg = oht_ref.shape[0]
    onehot = (iota((count_agg, block), 0) == agg_ref[...]).astype(f32)
    oht_ref[...] = onehot.astype(bf16)
    oh_ref[...] = onehot.T.astype(bf16)


def run_setup(fine_values, columns, agg_map, block, aggregates):
    entries, rows = fine_values.shape
    blocks = rows // block
    return pl.pallas_call(
        setup_kernel,
        grid=(blocks,),
        in_specs=[
            pl.BlockSpec((entries, block), lambda b: (0, b)),
            pl.BlockSpec((entries, block), lambda b: (0, b)),
            pl.BlockSpec((1, block), lambda b: (0, b)),
        ],
        out_specs=[
            pl.BlockSpec((2 * block, 2 * block), lambda b: (b, 0)),
            pl.BlockSpec((block, block), lambda b: (b, 0)),
            pl.BlockSpec((block, block), lambda b: (b, 0)),
            pl.BlockSpec((aggregates, block), lambda b: (0, b)),
            pl.BlockSpec((block, aggregates), lambda b: (b, 0)),
        ],
        out_shape=[
            jax.ShapeDtypeStruct((2 * rows, 2 * block), bf16),
            jax.ShapeDtypeStruct((rows, block), f32),
            jax.ShapeDtypeStruct((rows, block), f32),
            jax.ShapeDtypeStruct((aggregates, rows), bf16),
            jax.ShapeDtypeStruct((rows, aggregates), bf16),
        ],
        cost_estimate=pl.CostEstimate(flops=10_000_000_000, bytes_accessed=50_000_000, transcendentals=0),
        name="setup",
    )(fine_values, columns, agg_map.reshape(1, rows))


def poly_kernel(m_ref, out_ref, m_hi, m_lo, d_ref, z_ref, x_ref, pair):
    coarse = m_ref.shape[0]
    agg = x_ref.shape[0]
    parts = coarse // agg
    half = parts // 2
    me = lax.axis_index("sub")
    eye = iota((agg, agg), 0) == iota((agg, agg), 1)
    cinv = []
    for j in range(coarse // agg):
        sl = slice(j * agg, (j + 1) * agg)
        cinv.append(1.0 / jnp.sum(jnp.where(eye, m_ref[sl, :agg], 0.0), axis=0, keepdims=True))
        for k in range(half + 1):
            other = (j + k) % parts
            so = slice(other * agg, (other + 1) * agg)
            tile = m_ref[sl, k * agg : (k + 1) * agg]
            m_hi[sl, so], m_lo[sl, so] = split(tile)
            if 0 < k and 2 * k < parts:
                m_hi[so, sl], m_lo[so, sl] = split(tile.T)
    for j in range(coarse // agg):
        sl = slice(j * agg, (j + 1) * agg)
        start = jnp.where(jnp.logical_and(eye, me == j), cinv[j], 0.0)
        d_ref[:, sl] = start
        z_ref[:, sl] = start
        x_ref[:, sl] = start
    rho_old = DELTA / THETA
    for turn in range(1, CHEB_COARSE):
        rho_new = 1.0 / (2.0 * THETA / DELTA - rho_old)
        hi, lo = split(d_ref[...])
        pair[:agg, :] = hi
        pair[agg:, :] = lo
        for j in range(coarse // agg // 2):
            sl = slice(2 * j * agg, (2 * j + 2) * agg)
            both = jnp.dot(pair[...], m_hi[:, sl], preferred_element_type=f32)
            low = jnp.dot(pair[:agg, :], m_lo[:, sl], preferred_element_type=f32)
            scale = jnp.concatenate([cinv[2 * j], cinv[2 * j + 1]], axis=1)
            z = z_ref[:, sl] - (both[:agg] + (both[agg:] + low)) * scale
            d = rho_new * rho_old * d_ref[:, sl] + (2.0 * rho_new / DELTA) * z
            z_ref[:, sl] = z
            d_ref[:, sl] = d
            x_ref[:, sl] += d
        rho_old = rho_new
    hi, lo = split(x_ref[...])
    out_ref[:agg, :] = hi
    out_ref[agg:, :] = lo


def run_poly(matrix, agg):
    coarse = matrix.shape[0]
    vmem = pl.BlockSpec(memory_space=pltpu.VMEM)
    return pl.pallas_call(
        poly_kernel,
        in_specs=[vmem],
        out_specs=vmem,
        out_shape=jax.ShapeDtypeStruct((2 * agg, coarse), bf16),
        scratch_shapes=[
            pltpu.VMEM((coarse, coarse), bf16),
            pltpu.VMEM((coarse, coarse), bf16),
            pltpu.VMEM((agg, coarse), f32),
            pltpu.VMEM((agg, coarse), f32),
            pltpu.VMEM((agg, coarse), f32),
            pltpu.VMEM((2 * agg, coarse), bf16),
        ],
        compiler_params=pltpu.CompilerParams(vmem_limit_bytes=50 * 1024 * 1024),
        name="poly",
    )(matrix)


def quads(product, rows, width):
    return product[:rows, :width] + (product[:rows, width:] + product[rows:, :width])


def main_kernel(opening, n_grp, n_sub, *refs):
    if opening:
        (rhs_ref, a_ref, dinv_ref, oht_ref, lo_ref, hi_ref,
         sol_ref, res_ref, crhs_ref,
         xs, ext, s2, send, recv, send_sem, recv_sem) = refs
        agg = oht_ref.shape[0]
    else:
        (sol_in, rhs_ref, crhs_ref, a_ref, dinv_ref, diag_ref, oht_ref, oh_ref, lo_ref, hi_ref, m2,
         sol_ref, res_ref,
         xs, ext, s2, send, recv, send_sem, recv_sem,
         csend, whole, csend_sem, crecv_sem) = refs
        agg = oht_ref.shape[0]
    rows_dev, width = rhs_ref.shape
    ghost = lo_ref.shape[0]
    block = 2 * ghost
    blocks = rows_dev // block
    grp = lax.axis_index("grp")
    me = lax.axis_index("sub")
    part = grp * n_sub + me
    has_next = part < n_grp * n_sub - 1
    has_prev = part > 0
    after, before = part + 1, part - 1
    next_id = (lax.div(after, n_sub), lax.rem(after, n_sub))
    prev_id = (lax.div(before, n_sub), lax.rem(before, n_sub))
    cross_next = jnp.logical_and(has_next, me == n_sub - 1)
    cross_prev = jnp.logical_and(has_prev, me == 0)

    barrier = pltpu.get_barrier_semaphore()
    if opening:
        greet_next, greet_prev, greeted = has_next, has_prev, 0
    else:
        greet_next, greet_prev, greeted = cross_next, cross_prev, n_sub - 1
        for j in range(1, n_sub):
            pl.semaphore_signal(barrier, inc=1, device_id=(grp, lax.rem(me + j, n_sub)), device_id_type=MESH)

    @pl.when(greet_next)
    def _():
        pl.semaphore_signal(barrier, inc=1, device_id=next_id, device_id_type=MESH)

    @pl.when(greet_prev)
    def _():
        pl.semaphore_signal(barrier, inc=1, device_id=prev_id, device_id_type=MESH)

    mine = pl.multiple_of(me * agg, agg)
    ext[:ghost, :] = jnp.zeros((ghost, 2 * width), bf16)
    ext[ghost + rows_dev :, :] = jnp.zeros((ghost, 2 * width), bf16)

    def each_block(fn):
        def go(b, carry):
            fn(pl.ds(pl.multiple_of(b * block, block), block))
            return carry
        lax.fori_loop(0, blocks, go, 0, unroll=True)

    def first(sl):
        rhs = rhs_ref[sl, :]
        res_ref[sl, :] = rhs
        if opening:
            sol_ref[sl, :] = jnp.zeros_like(rhs)
            xs[0, sl, :] = dinv_ref[sl, :] * rhs
        else:
            sol_ref[sl, :] = sol_in[sl, :]

    each_block(first)
    pl.semaphore_wait(barrier, greeted + greet_next.astype(jnp.int32) + greet_prev.astype(jnp.int32))

    def halo_copy(ex, way, device):
        return pltpu.make_async_remote_copy(
            src_ref=send.at[ex, way], dst_ref=recv.at[ex, way],
            send_sem=send_sem.at[ex, way], recv_sem=recv_sem.at[ex, way],
            device_id=device, device_id_type=MESH,
        )

    def apply(ex, cur, epilogue):
        up = halo_copy(ex, 0, next_id)
        down = halo_copy(ex, 1, prev_id)

        @pl.when(has_next)
        def _():
            def pick(i, carry):
                for k in range(16):
                    send[ex, 0, pl.ds(16 * i + k, 1), :] = xs[cur, pl.ds(hi_ref[16 * i + k], 1), :]
                return carry

            lax.fori_loop(0, ghost // 16, pick, 0)
            up.start()

        @pl.when(has_prev)
        def _():
            def pick(i, carry):
                for k in range(16):
                    send[ex, 1, pl.ds(16 * i + k, 1), :] = xs[cur, pl.ds(lo_ref[16 * i + k], 1), :]
                return carry

            lax.fori_loop(0, ghost // 16, pick, 0)
            down.start()

        for b in range(blocks):
            hi, lo = split(xs[cur, b * block : (b + 1) * block, :])
            at = ghost + b * block
            ext[at : at + block, :width] = hi
            ext[at : at + block, width:] = lo

        def one(b):
            a = a_ref[pl.ds(pl.multiple_of(b * 2 * block, 2 * block), 2 * block), :]
            x = ext[pl.ds(pl.multiple_of(b * block, block), 2 * block), :]
            off = quads(jnp.dot(a, x, preferred_element_type=f32), block, width)
            epilogue(pl.ds(pl.multiple_of(b * block, block), block), off)

        def go(b, carry):
            one(1 + 2 * b)
            one(2 + 2 * b)
            return carry

        lax.fori_loop(0, (blocks - 2) // 2, go, 0)

        @pl.when(has_next)
        def _():
            down.wait_recv()
            hi, lo = split(recv[ex, 1])
            ext[ghost + rows_dev :, :width] = hi
            ext[ghost + rows_dev :, width:] = lo
            up.wait_send()

        @pl.when(has_prev)
        def _():
            up.wait_recv()
            hi, lo = split(recv[ex, 0])
            ext[:ghost, :width] = hi
            ext[:ghost, width:] = lo
            down.wait_send()

        one(0)
        one(blocks - 1)

    def gather(step):
        copies = []
        for j in range(1, n_sub):
            copies.append(pltpu.make_async_remote_copy(
                src_ref=csend.at[step], dst_ref=whole.at[step, pl.ds(mine, agg)],
                send_sem=csend_sem.at[step, j], recv_sem=crecv_sem.at[step, j],
                device_id=(grp, lax.rem(me + j, n_sub)), device_id_type=MESH,
            ))
        for copy in copies:
            copy.start()
        whole[step, pl.ds(mine, agg), :] = csend[step]
        for copy in copies:
            copy.wait()
        hi, lo = split(whole[step])
        x = jnp.concatenate([hi, lo], axis=1)
        return quads(jnp.dot(m2[...], x, preferred_element_type=f32), agg, width)

    rho0 = DELTA / THETA
    rho1 = 1.0 / (2.0 * THETA / DELTA - rho0)
    c1 = rho1 * rho0
    c2 = 2.0 * rho1 / DELTA

    def smooth(ex):
        def step_one(sl, off):
            d0 = xs[0, sl, :]
            r0 = res_ref[sl, :]
            d1 = c1 * d0 - c2 * dinv_ref[sl, :] * off
            xs[1, sl, :] = d1
            res_ref[sl, :] = (c2 - 1.0) * off - c1 * r0
            sol_ref[sl, :] += d0 + d1

        apply(ex, 0, step_one)

        def step_two(sl, off):
            r = res_ref[sl, :] - off
            res_ref[sl, :] = r
            xs[0, sl, :] = dinv_ref[sl, :] * r

        apply(ex + 1, 1, step_two)

    def restrict(sl, off):
        s = (1.0 - OMEGA) * res_ref[sl, :] - OMEGA * off
        hi, lo = split(s)
        s2[sl, :width] = hi
        s2[sl, width:] = lo

    def restricted(ex):
        apply(ex, 0, restrict)
        both = jnp.dot(oht_ref[...], s2[...], preferred_element_type=f32)
        return both[:, :width] + both[:, width:]

    if opening:
        smooth(0)
        crhs_ref[...] = restricted(2)
        return

    csend[0] = crhs_ref[...]

    def cycle_body(cycle, carry):
        ex = cycle * APPLIES
        hi, lo = split(gather(cycle))
        packed = jnp.concatenate([hi, lo], axis=1)

        def spread(sl):
            both = jnp.dot(oh_ref[sl, :], packed, preferred_element_type=f32)
            xs[0, sl, :] = both[:, :width] + both[:, width:]

        each_block(spread)

        def prolong(sl, off):
            e = (1.0 - OMEGA) * xs[0, sl, :] - OMEGA * (dinv_ref[sl, :] * off)
            xs[1, sl, :] = e
            sol_ref[sl, :] += e

        apply(ex, 0, prolong)

        def correct(sl, off):
            r = res_ref[sl, :] - (diag_ref[sl, :] * xs[1, sl, :] + off)
            res_ref[sl, :] = r
            xs[0, sl, :] = dinv_ref[sl, :] * r

        apply(ex + 1, 1, correct)
        smooth(ex + 2)

        @pl.when(cycle < CYCLES - 1)
        def _():
            smooth(ex + 4)
            csend[cycle + 1] = restricted(ex + 6)

        return carry

    lax.fori_loop(0, CYCLES, cycle_body, 0)


def body(n_grp, n_sub, right_side, fine_values, columns, agg_map, send_lo, send_hi, coarse_matrix):
    rows, width = right_side.shape
    ghost = send_lo.shape[0]
    block = 2 * ghost
    own = coarse_matrix[0]
    agg, coarse = own.shape
    a2, dinv, diag, oht, oh = run_setup(fine_values, columns, agg_map, block, agg)
    start = lax.axis_index("sub") * agg
    kept = (coarse // agg // 2 + 1) * agg
    slab = lax.dynamic_slice_in_dim(jnp.concatenate([own, own], 1), start, kept, 1)
    matrix = lax.all_gather(slab, "sub", axis=0, tiled=True)
    vmem = pl.BlockSpec(memory_space=pltpu.VMEM)
    smem = pl.BlockSpec(memory_space=pltpu.SMEM)
    field = jax.ShapeDtypeStruct((rows, width), f32)

    def scratch(exchanges):
        return [
            pltpu.VMEM((2, rows, width), f32),
            pltpu.VMEM((rows + block, 2 * width), bf16),
            pltpu.VMEM((rows, 2 * width), bf16),
            pltpu.VMEM((exchanges, 2, ghost, width), f32),
            pltpu.VMEM((exchanges, 2, ghost, width), f32),
            pltpu.SemaphoreType.DMA((exchanges, 2)),
            pltpu.SemaphoreType.DMA((exchanges, 2)),
        ]

    def params(number):
        return pltpu.CompilerParams(
            collective_id=number, has_side_effects=True, vmem_limit_bytes=50 * 1024 * 1024
        )

    sol, res, crhs = pl.pallas_call(
        functools.partial(main_kernel, True, n_grp, n_sub),
        in_specs=[vmem] * 4 + [smem] * 2,
        out_specs=[vmem] * 3,
        out_shape=[field, field, jax.ShapeDtypeStruct((agg, width), f32)],
        scratch_shapes=scratch(3),
        compiler_params=params(0),
        cost_estimate=pl.CostEstimate(flops=20_000_000_000, bytes_accessed=60_000_000, transcendentals=0),
        name="opening",
    )(right_side, a2, dinv, oht, send_lo, send_hi)
    p2 = run_poly(matrix, agg)
    return pl.pallas_call(
        functools.partial(main_kernel, False, n_grp, n_sub),
        in_specs=[vmem] * 8 + [smem] * 2 + [vmem],
        out_specs=[vmem] * 2,
        out_shape=[field] * 2,
        scratch_shapes=scratch(CYCLES * APPLIES - 3) + [
            pltpu.VMEM((CYCLES, agg, width), f32),
            pltpu.VMEM((CYCLES, coarse, width), f32),
            pltpu.SemaphoreType.DMA((CYCLES, n_sub)),
            pltpu.SemaphoreType.DMA((CYCLES, n_sub)),
        ],
        compiler_params=params(1),
        name="cycles",
    )(sol, res, crhs, a2, dinv, diag, oht, oh, send_lo, send_hi, p2)


def solution(mesh):
    placed = (
        P(("grp", "sub"), None),
        P(None, ("grp", "sub")),
        P(None, ("grp", "sub")),
        P(("grp", "sub")),
        P(("grp", "sub")),
        P(("grp", "sub")),
        P("grp", "sub", None),
    )
    return jax.shard_map(
        functools.partial(body, mesh.shape["grp"], mesh.shape["sub"]),
        mesh=mesh,
        in_specs=placed,
        out_specs=(P(("grp", "sub"), None), P(("grp", "sub"), None)),
        check_vma=False,
    )
```

```python
import functools

import jax
import jax.numpy as jnp
from jax import lax
from jax.experimental import pallas as pl
from jax.experimental.pallas import tpu as pltpu
from jax.sharding import PartitionSpec as P

CHEB_FINE = 2
CHEB_COARSE = 6
CYCLES = 2
APPLIES = 7

THETA = 1.0
DELTA = 0.7
OMEGA = 0.6
MESH = pl.DeviceIdType.MESH
f32 = jnp.float32
bf16 = jnp.bfloat16


def split(x):
    hi = x.astype(bf16)
    lo = (x - hi.astype(f32)).astype(bf16)
    return hi, lo


def iota(shape, dim):
    return lax.broadcasted_iota(jnp.int32, shape, dim)


def setup_kernel(fv_ref, col_ref, agg_ref, a_ref, dinv_ref, diag_ref, oht_ref, oh_ref):
    block = fv_ref.shape[1]
    count = fv_ref.shape[0] - 1
    groups = count // 8
    base = pl.program_id(0) * block
    rows = iota((8, block), 1)
    cols, vals, firsts = [], [], []
    for i in range(groups):
        cols.append(col_ref[1 + 8 * i : 9 + 8 * i, :] - base - rows)
        vals.append(fv_ref[1 + 8 * i : 9 + 8 * i, :])
    last = jnp.zeros((8, block), f32)
    for i in range(groups):
        last = last + jnp.where(cols[i] == block, vals[i], 0.0)
    last = jnp.sum(last, axis=0, keepdims=True)
    for j in range(groups):
        total = vals[j]
        for i in range(j + 1, groups):
            total = total + jnp.where(cols[i] == cols[j], vals[i], 0.0)
        firsts.append(total)
    high_count = block // 8
    places = [iota((8, block), 0) + 8 * h for h in range(high_count)]
    sums = [jnp.zeros((8, block), f32)] * high_count
    for s in range(8):
        chains = [jnp.zeros((8, block), f32)] * high_count
        for i in reversed(range(groups)):
            col = jnp.broadcast_to(cols[i][s : s + 1, :], (8, block))
            val = jnp.broadcast_to(firsts[i][s : s + 1, :], (8, block))
            chains = [jnp.where(col == places[h], val, chains[h]) for h in range(high_count)]
        sums = [sums[h] + chains[h] for h in range(high_count)]
    by_offset = jnp.concatenate(sums, axis=0).T
    skewed = pltpu.roll(by_offset, 0, 1, stride=1, stride_axis=0)
    lane = iota((block, block), 1)
    sub = iota((block, block), 0)
    low = jnp.where(lane >= sub, skewed, 0.0)
    high = jnp.where(lane < sub, skewed, jnp.where(lane == sub, last, 0.0))
    for part, at in ((low, 0), (high, block)):
        hi, lo = split(part)
        a_ref[:block, at : at + block] = hi
        a_ref[block:, at : at + block] = lo
    diag = jnp.broadcast_to(fv_ref[0:1, :], (block, block)).T
    diag_ref[...] = diag
    dinv_ref[...] = 1.0 / diag
    count_agg = oht_ref.shape[0]
    onehot = (iota((count_agg, block), 0) == agg_ref[...]).astype(f32)
    oht_ref[...] = onehot.astype(bf16)
    oh_ref[...] = onehot.T.astype(bf16)


def run_setup(fine_values, columns, agg_map, block, aggregates):
    entries, rows = fine_values.shape
    blocks = rows // block
    return pl.pallas_call(
        setup_kernel,
        grid=(blocks,),
        in_specs=[
            pl.BlockSpec((entries, block), lambda b: (0, b)),
            pl.BlockSpec((entries, block), lambda b: (0, b)),
            pl.BlockSpec((1, block), lambda b: (0, b)),
        ],
        out_specs=[
            pl.BlockSpec((2 * block, 2 * block), lambda b: (b, 0)),
            pl.BlockSpec((block, block), lambda b: (b, 0)),
            pl.BlockSpec((block, block), lambda b: (b, 0)),
            pl.BlockSpec((aggregates, block), lambda b: (0, b)),
            pl.BlockSpec((block, aggregates), lambda b: (b, 0)),
        ],
        out_shape=[
            jax.ShapeDtypeStruct((2 * rows, 2 * block), bf16),
            jax.ShapeDtypeStruct((rows, block), f32),
            jax.ShapeDtypeStruct((rows, block), f32),
            jax.ShapeDtypeStruct((aggregates, rows), bf16),
            jax.ShapeDtypeStruct((rows, aggregates), bf16),
        ],
        cost_estimate=pl.CostEstimate(flops=10_000_000_000, bytes_accessed=50_000_000, transcendentals=0),
        name="setup",
    )(fine_values, columns, agg_map.reshape(1, rows))


def poly_kernel(m_ref, out_ref, m_hi, m_lo, d_ref, z_ref, x_ref, pair):
    coarse = m_ref.shape[0]
    agg = x_ref.shape[0]
    parts = coarse // agg
    half = parts // 2
    me = lax.axis_index("sub")
    eye = iota((agg, agg), 0) == iota((agg, agg), 1)
    cinv = []
    for j in range(coarse // agg):
        sl = slice(j * agg, (j + 1) * agg)
        cinv.append(1.0 / jnp.sum(jnp.where(eye, m_ref[sl, :agg], 0.0), axis=0, keepdims=True))
        for k in range(half + 1):
            other = (j + k) % parts
            so = slice(other * agg, (other + 1) * agg)
            tile = m_ref[sl, k * agg : (k + 1) * agg]
            m_hi[sl, so], m_lo[sl, so] = split(tile)
            if 0 < k and 2 * k < parts:
                m_hi[so, sl], m_lo[so, sl] = split(tile.T)
    for j in range(coarse // agg):
        sl = slice(j * agg, (j + 1) * agg)
        start = jnp.where(jnp.logical_and(eye, me == j), cinv[j], 0.0)
        d_ref[:, sl] = start
        z_ref[:, sl] = start
        x_ref[:, sl] = start
    rho_old = DELTA / THETA
    for turn in range(1, CHEB_COARSE):
        rho_new = 1.0 / (2.0 * THETA / DELTA - rho_old)
        hi, lo = split(d_ref[...])
        pair[:agg, :] = hi
        pair[agg:, :] = lo
        for j in range(coarse // agg // 2):
            sl = slice(2 * j * agg, (2 * j + 2) * agg)
            both = jnp.dot(pair[...], m_hi[:, sl], preferred_element_type=f32)
            low = jnp.dot(pair[:agg, :], m_lo[:, sl], preferred_element_type=f32)
            scale = jnp.concatenate([cinv[2 * j], cinv[2 * j + 1]], axis=1)
            z = z_ref[:, sl] - (both[:agg] + (both[agg:] + low)) * scale
            d = rho_new * rho_old * d_ref[:, sl] + (2.0 * rho_new / DELTA) * z
            z_ref[:, sl] = z
            d_ref[:, sl] = d
            x_ref[:, sl] += d
        rho_old = rho_new
    hi, lo = split(x_ref[...])
    out_ref[:agg, :] = hi
    out_ref[agg:, :] = lo


def run_poly(matrix, agg):
    coarse = matrix.shape[0]
    vmem = pl.BlockSpec(memory_space=pltpu.VMEM)
    return pl.pallas_call(
        poly_kernel,
        in_specs=[vmem],
        out_specs=vmem,
        out_shape=jax.ShapeDtypeStruct((2 * agg, coarse), bf16),
        scratch_shapes=[
            pltpu.VMEM((coarse, coarse), bf16),
            pltpu.VMEM((coarse, coarse), bf16),
            pltpu.VMEM((agg, coarse), f32),
            pltpu.VMEM((agg, coarse), f32),
            pltpu.VMEM((agg, coarse), f32),
            pltpu.VMEM((2 * agg, coarse), bf16),
        ],
        compiler_params=pltpu.CompilerParams(vmem_limit_bytes=50 * 1024 * 1024),
        name="poly",
    )(matrix)


def quads(product, rows, width):
    return product[:rows, :width] + (product[:rows, width:] + product[rows:, :width])


def main_kernel(opening, n_grp, n_sub, *refs):
    if opening:
        (rhs_ref, a_ref, dinv_ref, oht_ref, lo_ref, hi_ref,
         sol_ref, res_ref, crhs_ref,
         xs, ext, s2, send, recv, send_sem, recv_sem) = refs
        agg = oht_ref.shape[0]
    else:
        (sol_in, rhs_ref, crhs_ref, a_ref, dinv_ref, diag_ref, oht_ref, oh_ref, lo_ref, hi_ref, m2,
         sol_ref, res_ref,
         xs, ext, s2, send, recv, send_sem, recv_sem,
         csend, whole, csend_sem, crecv_sem) = refs
        agg = oht_ref.shape[0]
    rows_dev, width = rhs_ref.shape
    ghost = lo_ref.shape[0]
    block = 2 * ghost
    blocks = rows_dev // block
    grp = lax.axis_index("grp")
    me = lax.axis_index("sub")
    part = grp * n_sub + me
    has_next = part < n_grp * n_sub - 1
    has_prev = part > 0
    after, before = part + 1, part - 1
    next_id = (lax.div(after, n_sub), lax.rem(after, n_sub))
    prev_id = (lax.div(before, n_sub), lax.rem(before, n_sub))
    cross_next = jnp.logical_and(has_next, me == n_sub - 1)
    cross_prev = jnp.logical_and(has_prev, me == 0)

    barrier = pltpu.get_barrier_semaphore()
    if opening:
        greet_next, greet_prev, greeted = has_next, has_prev, 0
    else:
        greet_next, greet_prev, greeted = cross_next, cross_prev, n_sub - 1
        for j in range(1, n_sub):
            pl.semaphore_signal(barrier, inc=1, device_id=(grp, lax.rem(me + j, n_sub)), device_id_type=MESH)

    @pl.when(greet_next)
    def _():
        pl.semaphore_signal(barrier, inc=1, device_id=next_id, device_id_type=MESH)

    @pl.when(greet_prev)
    def _():
        pl.semaphore_signal(barrier, inc=1, device_id=prev_id, device_id_type=MESH)

    mine = pl.multiple_of(me * agg, agg)
    ext[:ghost, :] = jnp.zeros((ghost, 2 * width), bf16)
    ext[ghost + rows_dev :, :] = jnp.zeros((ghost, 2 * width), bf16)

    def each_block(fn):
        def go(b, carry):
            fn(pl.ds(pl.multiple_of(b * block, block), block))
            return carry
        lax.fori_loop(0, blocks, go, 0, unroll=True)

    def first(sl):
        rhs = rhs_ref[sl, :]
        res_ref[sl, :] = rhs
        if opening:
            sol_ref[sl, :] = jnp.zeros_like(rhs)
            xs[0, sl, :] = dinv_ref[sl, :] * rhs
        else:
            sol_ref[sl, :] = sol_in[sl, :]

    each_block(first)
    pl.semaphore_wait(barrier, greeted + greet_next.astype(jnp.int32) + greet_prev.astype(jnp.int32))

    def halo_copy(ex, way, device):
        return pltpu.make_async_remote_copy(
            src_ref=send.at[ex, way], dst_ref=recv.at[ex, way],
            send_sem=send_sem.at[ex, way], recv_sem=recv_sem.at[ex, way],
            device_id=device, device_id_type=MESH,
        )

    def apply(ex, cur, epilogue):
        up = halo_copy(ex, 0, next_id)
        down = halo_copy(ex, 1, prev_id)

        @pl.when(has_next)
        def _():
            def pick(i, carry):
                for k in range(16):
                    send[ex, 0, pl.ds(16 * i + k, 1), :] = xs[cur, pl.ds(hi_ref[16 * i + k], 1), :]
                return carry

            lax.fori_loop(0, ghost // 16, pick, 0)
            up.start()

        @pl.when(has_prev)
        def _():
            def pick(i, carry):
                for k in range(16):
                    send[ex, 1, pl.ds(16 * i + k, 1), :] = xs[cur, pl.ds(lo_ref[16 * i + k], 1), :]
                return carry

            lax.fori_loop(0, ghost // 16, pick, 0)
            down.start()

        for b in range(blocks):
            hi, lo = split(xs[cur, b * block : (b + 1) * block, :])
            at = ghost + b * block
            ext[at : at + block, :width] = hi
            ext[at : at + block, width:] = lo

        def one(b):
            a = a_ref[pl.ds(pl.multiple_of(b * 2 * block, 2 * block), 2 * block), :]
            x = ext[pl.ds(pl.multiple_of(b * block, block), 2 * block), :]
            off = quads(jnp.dot(a, x, preferred_element_type=f32), block, width)
            epilogue(pl.ds(pl.multiple_of(b * block, block), block), off)

        def go(b, carry):
            one(1 + 2 * b)
            one(2 + 2 * b)
            return carry

        lax.fori_loop(0, (blocks - 2) // 2, go, 0)

        @pl.when(has_next)
        def _():
            down.wait_recv()
            hi, lo = split(recv[ex, 1])
            ext[ghost + rows_dev :, :width] = hi
            ext[ghost + rows_dev :, width:] = lo
            up.wait_send()

        @pl.when(has_prev)
        def _():
            up.wait_recv()
            hi, lo = split(recv[ex, 0])
            ext[:ghost, :width] = hi
            ext[:ghost, width:] = lo
            down.wait_send()

        one(0)
        one(blocks - 1)

    def gather(step):
        half = n_sub // 2
        partner = me + 1 - 2 * lax.rem(me, 2)

        def block_copy(source, origin, slot, peer):
            return pltpu.make_async_remote_copy(
                src_ref=source, dst_ref=whole.at[step, pl.ds(pl.multiple_of(origin * agg, agg), agg)],
                send_sem=csend_sem.at[step, slot], recv_sem=crecv_sem.at[step, slot],
                device_id=(grp, peer), device_id_type=MESH,
            )

        copies = [block_copy(csend.at[step], me, 0, partner)]
        for j in range(1, half):
            copies.append(block_copy(csend.at[step], me, j, lax.rem(me + 2 * j, n_sub)))
        for copy in copies:
            copy.start()
        whole[step, pl.ds(mine, agg), :] = csend[step]
        passed = []
        for j in range(1, half):
            copies[j].wait_recv()
            origin = lax.rem(me + n_sub - 2 * j, n_sub)
            block_ref = whole.at[step, pl.ds(pl.multiple_of(origin * agg, agg), agg)]
            copy = block_copy(block_ref, origin, half + j, partner)
            copy.start()
            passed.append(copy)
        copies[0].wait_recv()
        for copy in passed:
            copy.wait_recv()
        for copy in copies + passed:
            copy.wait_send()
        hi, lo = split(whole[step])
        x = jnp.concatenate([hi, lo], axis=1)
        return quads(jnp.dot(m2[...], x, preferred_element_type=f32), agg, width)

    rho0 = DELTA / THETA
    rho1 = 1.0 / (2.0 * THETA / DELTA - rho0)
    c1 = rho1 * rho0
    c2 = 2.0 * rho1 / DELTA

    def smooth(ex):
        def step_one(sl, off):
            d0 = xs[0, sl, :]
            r0 = res_ref[sl, :]
            d1 = c1 * d0 - c2 * dinv_ref[sl, :] * off
            xs[1, sl, :] = d1
            res_ref[sl, :] = (c2 - 1.0) * off - c1 * r0
            sol_ref[sl, :] += d0 + d1

        apply(ex, 0, step_one)

        def step_two(sl, off):
            r = res_ref[sl, :] - off
            res_ref[sl, :] = r
            xs[0, sl, :] = dinv_ref[sl, :] * r

        apply(ex + 1, 1, step_two)

    def restrict(sl, off):
        s = (1.0 - OMEGA) * res_ref[sl, :] - OMEGA * off
        hi, lo = split(s)
        s2[sl, :width] = hi
        s2[sl, width:] = lo

    def restricted(ex):
        apply(ex, 0, restrict)
        both = jnp.dot(oht_ref[...], s2[...], preferred_element_type=f32)
        return both[:, :width] + both[:, width:]

    if opening:
        smooth(0)
        crhs_ref[...] = restricted(2)
        return

    csend[0] = crhs_ref[...]

    def cycle_body(cycle, carry):
        ex = cycle * APPLIES
        hi, lo = split(gather(cycle))
        packed = jnp.concatenate([hi, lo], axis=1)

        def spread(sl):
            both = jnp.dot(oh_ref[sl, :], packed, preferred_element_type=f32)
            xs[0, sl, :] = both[:, :width] + both[:, width:]

        each_block(spread)

        def prolong(sl, off):
            e = (1.0 - OMEGA) * xs[0, sl, :] - OMEGA * (dinv_ref[sl, :] * off)
            xs[1, sl, :] = e
            sol_ref[sl, :] += e

        apply(ex, 0, prolong)

        def correct(sl, off):
            r = res_ref[sl, :] - (diag_ref[sl, :] * xs[1, sl, :] + off)
            res_ref[sl, :] = r
            xs[0, sl, :] = dinv_ref[sl, :] * r

        apply(ex + 1, 1, correct)
        smooth(ex + 2)

        @pl.when(cycle < CYCLES - 1)
        def _():
            smooth(ex + 4)
            csend[cycle + 1] = restricted(ex + 6)

        return carry

    lax.fori_loop(0, CYCLES, cycle_body, 0)


def body(n_grp, n_sub, right_side, fine_values, columns, agg_map, send_lo, send_hi, coarse_matrix):
    rows, width = right_side.shape
    ghost = send_lo.shape[0]
    block = 2 * ghost
    own = coarse_matrix[0]
    agg, coarse = own.shape
    a2, dinv, diag, oht, oh = run_setup(fine_values, columns, agg_map, block, agg)
    start = lax.axis_index("sub") * agg
    kept = (coarse // agg // 2 + 1) * agg
    slab = lax.dynamic_slice_in_dim(jnp.concatenate([own, own], 1), start, kept, 1)
    matrix = lax.all_gather(slab, "sub", axis=0, tiled=True)
    vmem = pl.BlockSpec(memory_space=pltpu.VMEM)
    smem = pl.BlockSpec(memory_space=pltpu.SMEM)
    field = jax.ShapeDtypeStruct((rows, width), f32)

    def scratch(exchanges):
        return [
            pltpu.VMEM((2, rows, width), f32),
            pltpu.VMEM((rows + block, 2 * width), bf16),
            pltpu.VMEM((rows, 2 * width), bf16),
            pltpu.VMEM((exchanges, 2, ghost, width), f32),
            pltpu.VMEM((exchanges, 2, ghost, width), f32),
            pltpu.SemaphoreType.DMA((exchanges, 2)),
            pltpu.SemaphoreType.DMA((exchanges, 2)),
        ]

    def params(number):
        return pltpu.CompilerParams(
            collective_id=number, has_side_effects=True, vmem_limit_bytes=50 * 1024 * 1024
        )

    sol, res, crhs = pl.pallas_call(
        functools.partial(main_kernel, True, n_grp, n_sub),
        in_specs=[vmem] * 4 + [smem] * 2,
        out_specs=[vmem] * 3,
        out_shape=[field, field, jax.ShapeDtypeStruct((agg, width), f32)],
        scratch_shapes=scratch(3),
        compiler_params=params(0),
        cost_estimate=pl.CostEstimate(flops=20_000_000_000, bytes_accessed=60_000_000, transcendentals=0),
        name="opening",
    )(right_side, a2, dinv, oht, send_lo, send_hi)
    p2 = run_poly(matrix, agg)
    return pl.pallas_call(
        functools.partial(main_kernel, False, n_grp, n_sub),
        in_specs=[vmem] * 8 + [smem] * 2 + [vmem],
        out_specs=[vmem] * 2,
        out_shape=[field] * 2,
        scratch_shapes=scratch(CYCLES * APPLIES - 3) + [
            pltpu.VMEM((CYCLES, agg, width), f32),
            pltpu.VMEM((CYCLES, coarse, width), f32),
            pltpu.SemaphoreType.DMA((CYCLES, n_sub)),
            pltpu.SemaphoreType.DMA((CYCLES, n_sub)),
        ],
        compiler_params=params(1),
        name="cycles",
    )(sol, res, crhs, a2, dinv, diag, oht, oh, send_lo, send_hi, p2)


def solution(mesh):
    placed = (
        P(("grp", "sub"), None),
        P(None, ("grp", "sub")),
        P(None, ("grp", "sub")),
        P(("grp", "sub")),
        P(("grp", "sub")),
        P(("grp", "sub")),
        P("grp", "sub", None),
    )
    return jax.shard_map(
        functools.partial(body, mesh.shape["grp"], mesh.shape["sub"]),
        mesh=mesh,
        in_specs=placed,
        out_specs=(P(("grp", "sub"), None), P(("grp", "sub"), None)),
        check_vma=False,
    )
```
